256 devices in a mesh: row: 8 (over z), col: 32 (over y, x, core).
Axes of the slice: x: 4, y: 4, z: 8, core: 2. Of those that a mesh axis runs over, the one named last changes fastest.
Arguments:
- out_grads: bfloat16 [32, 48, 28672], P('col', None, 'row'), may hold values from -6 to 6
- acts: bfloat16 [32, 48, 8192], P('row', None, 'col'), may hold values from -6 to 6
- rot_out: bfloat16 [28672, 28672], P('row', 'col'), may hold values from -0.03125 to 0.03125
- rot_in: bfloat16 [8192, 8192], P('col', 'row'), may hold values from -0.0625 to 0.0625
- queries: bfloat16 [2, 28672, 8192], P(None, 'col', 'row'), may hold values from -0.00036621094 to 0.00036621094
- token_sequence: int32 [1024], replicated, may hold values from 0 to 31, never falling along the last dimension, each value on 1 to 48 neighbouring positions
Outputs:
- scores: float32 [1024, 2], P(('row', 'col'))
The draws below stay inside these ranges and needn't reach their ends.
Inputs may be any that keep to these rules, and one draw needn't show every extreme that they name: `token_sequence`: values never fall along the tokens; every sequence 0 to 31 has 1 to 48 tokens, some sequence exactly 48; the k-th token of a sequence (from 0) sits in its slot k of out_grads and acts.
All inputs are finite; a program needn't handle non-finite values.
Results may differ from the reference program's by a relative error of at most 0.0041.
Values may be sent and summed in bfloat16 or wider, within the bound.
A program may use at most 128 MiB of HBM per device.

```python
import math
import jax
import jax.numpy as jnp
import numpy as np

DIN = 8192
DOUT = 28672
NQ = 2
SLOTS = 48
SEQS = 32
TOKENS = 1024


def level_of(rng, shape, split, low, high):
    gain = 1.0
    for axis_at, blocks in split:
        heights = jax.random.uniform(jax.random.fold_in(jax.random.fold_in(rng, 6), axis_at), (blocks,), jnp.float32, low / len(split), high / len(split))
        gain = gain * jnp.repeat(jnp.exp(heights), shape[axis_at] // blocks).reshape((-1,) + (1,) * (len(shape) - 1 - axis_at))
    return gain


def profile(count, total, bound, skew):
    weights = [(1 << 20) // math.isqrt(grade ** skew) + 1 for grade in range(2, count + 1)]
    rest, given = total - bound - (count - 1), [1] * (count - 1)
    while rest > 0:
        movable = [i for i in range(count - 1) if given[i] < bound]
        pool, left = sum([weights[i] for i in movable]), rest
        for i in movable:
            more = min(bound - given[i], max(1, left * weights[i] // pool), rest)
            given[i] = given[i] + more
            rest = rest - more
    return np.array([bound] + given)


def ragged_sizes(key, number_of, total, limit, skew):
    if number_of == 2:
        one = jax.random.randint(key, (), max(1, total - limit), min(limit, total - 1) + 1)
        return jnp.stack([one, total - one])
    lengths = jnp.asarray(profile(number_of, total, limit, skew), jnp.int32)
    couples = (number_of - 1) // 2
    giver, taker = lengths[1:1 + 2 * couples:2], lengths[2:2 + 2 * couples:2]
    room = jnp.minimum(giver - 1, limit - taker)
    shifted = jax.random.randint(jax.random.fold_in(key, 1), (couples,), 0, 1 << 20) % (room + 1)
    lengths = lengths.at[1:1 + 2 * couples:2].set(giver - shifted).at[2:2 + 2 * couples:2].set(taker + shifted)
    return lengths[jax.random.permutation(jax.random.fold_in(key, 2), number_of)]


def normal_values(key, dims, scale, reach, split=(), held_as=jnp.bfloat16):
    loudness = level_of(key, dims, split, -0.22, 0.18) if split else 1.0
    entries = jax.random.normal(key, dims, jnp.float32) * scale * loudness
    return jnp.minimum(jnp.maximum(entries, -reach), reach).astype(held_as)


def setup_inputs(seed: int = 0) -> dict:
    key_of = jax.random.split(jax.random.key(seed), 7)
    return {
        "out_grads": normal_values(key_of[0], (SEQS, SLOTS, DOUT), 1.0, 6.0, ((0, 32), (2, 8))),
        "acts": normal_values(key_of[1], (SEQS, SLOTS, DIN), 1.0, 6.0, ((0, 8), (2, 32))),
        "rot_out": normal_values(key_of[2], (DOUT, DOUT), DOUT ** -0.5, 0.03125, ((0, 8), (1, 32))),
        "rot_in": normal_values(key_of[3], (DIN, DIN), DIN ** -0.5, 0.0625, ((0, 32), (1, 8))),
        "queries": normal_values(key_of[4], (NQ, DOUT, DIN), (DOUT * DIN) ** -0.5, 0.00036621094, ((1, 32), (2, 8))),
        "token_sequence": jnp.searchsorted(jnp.cumsum(ragged_sizes(key_of[5], SEQS, TOKENS, SLOTS, 2)), jnp.arange(TOKENS), side="right").astype(jnp.int32),
    }


def token_places(token_sequence, seq_count, slot_count):
    token_count = token_sequence.shape[0]
    labels = jnp.arange(seq_count, dtype=jnp.int32)
    before = (token_sequence[:, None] < labels[None, :]).astype(jnp.int32)
    starts = jnp.sum(before, axis=0).astype(jnp.int32)
    member = (token_sequence[:, None] == labels[None, :]).astype(jnp.int32)
    own_start = jnp.sum(member * starts[None, :], axis=1).astype(jnp.int32)
    position = jnp.arange(token_count, dtype=jnp.int32) - own_start
    return (token_sequence * slot_count + position).astype(jnp.int32)


def reference(out_grads, acts, rot_out, rot_in, queries, token_sequence):
    flat_index = token_places(token_sequence, SEQS, SLOTS)
    grad_rows = out_grads.reshape(SEQS * SLOTS, DOUT)[flat_index]
    act_rows = acts.reshape(SEQS * SLOTS, DIN)[flat_index]
    rot_grads = jnp.dot(grad_rows, rot_out, preferred_element_type=jnp.float32).astype(jnp.bfloat16)
    rot_acts = jnp.dot(act_rows, rot_in, preferred_element_type=jnp.float32).astype(jnp.bfloat16)
    columns = []
    for query_index in range(NQ):
        projected = jnp.dot(rot_acts, queries[query_index].T, preferred_element_type=jnp.float32)
        columns.append(jnp.sum(rot_grads.astype(jnp.float32) * projected, axis=1))
    return jnp.stack(columns, axis=1)
```

```python
import jax
import jax.numpy as jnp
from jax import lax
from jax.experimental import pallas as pl
from jax.experimental.pallas import tpu as pltpu
from jax.sharding import Mesh
from jax.sharding import PartitionSpec as P

COL = ("col_0", "col_1", "col_2")
ROW_COL = ("row", "col_0", "col_1", "col_2")
MESH = pl.DeviceIdType.MESH
F32 = jnp.float32
BF16 = jnp.bfloat16
I32 = jnp.int32

RING = 4
ZED = 8
SLOTS = 48
SEQS = 32
PART = 128
HALF = 64
OFFSETS = (0, -1, 1, 2)
N_SEMS = 192


def ring4(i):
    return lax.rem(i + 8, 4)


def ring8(i):
    return lax.rem(i + 16, 8)


def kernel(
    grads, acts, rot_out_hbm, rot_in_hbm, queries_hbm, tokens, out,
    gbuf, wout, win, wq, hilo, parts, arrivals, rot_grads, abuf, rap, pair_in,
    e1_half, e1_full, e2_half, e2_full, rot_acts, proj, hot, nat, rel, mine, zsum, plane,
    send_sems, recv_sems, local_sems,
):
    z = lax.axis_index("row")
    y = lax.axis_index("col_0")
    x = lax.axis_index("col_1")
    k = lax.axis_index("col_2")
    o = 1 - k
    p1 = x * o + y * k
    p2 = y * o + x * k
    dout = wout.shape[1]
    half_in = wout.shape[0] // 2

    def first(d):
        return (z, ring4(y + k * d), ring4(x + o * d), k)

    def second(d):
        return (z, ring4(y + o * d), ring4(x + k * d), k)

    def along_z(d):
        return (ring8(z + d), y, x, k)

    sibling = (z, y, x, o)

    def along_x(d):
        return (z, y, ring4(x + d), k)

    def along_y(d):
        return (z, ring4(y + d), x, k)

    peers = [sibling] + [along_z(d) for d in range(1, 8)]
    peers += [along_x(d) for d in (1, 2, 3)] + [along_y(d) for d in (1, 2, 3)]
    barrier = pltpu.get_barrier_semaphore()
    for peer in peers:
        pl.semaphore_signal(barrier, inc=1, device_id=peer, device_id_type=MESH)
    pl.semaphore_wait(barrier, len(peers))

    started = []
    ids = {}

    def sem_id(name):
        return ids.setdefault(name, len(ids))

    def send(name, src, dst, to):
        i = sem_id(name)
        copy = pltpu.make_async_remote_copy(
            src_ref=src, dst_ref=dst, send_sem=send_sems.at[i], recv_sem=recv_sems.at[i],
            device_id=to, device_id_type=MESH,
        )
        copy.start()
        started.append(copy)

    def arrived(name, dst):
        i = sem_id(name)
        pltpu.make_async_remote_copy(
            src_ref=dst, dst_ref=dst, send_sem=send_sems.at[i], recv_sem=recv_sems.at[i],
            device_id=sibling, device_id_type=MESH,
        ).wait_recv()

    lo, hi = pl.ds(0, half_in), pl.ds(half_in, half_in)

    def block(j, i):
        return gbuf.at[j, k * 4 + ring4(p1 + OFFSETS[i])]

    def sibling_block(j, i):
        return gbuf.at[j, o * 4 + ring4(p2 + OFFSETS[i])]

    own = grads.at[0]
    send("g1+", own, block(0, 0), first(1))
    send("g1-", own, block(0, 0), first(-1))
    send("a+1", acts, abuf.at[z], along_z(1))
    send("a-1", acts, abuf.at[z], along_z(-1))
    send("s00", own, block(0, 0), sibling)
    keep = pltpu.make_async_copy(own, block(0, 0), local_sems.at[0])
    keep_acts = pltpu.make_async_copy(acts, abuf.at[z], local_sems.at[1])
    load_in = pltpu.make_async_copy(rot_in_hbm, win, local_sems.at[2])
    load_out = pltpu.make_async_copy(rot_out_hbm, wout, local_sems.at[3])
    load_q = pltpu.make_async_copy(queries_hbm, wq, local_sems.at[4])
    for copy in (keep, keep_acts, load_in, load_out, load_q):
        copy.start()

    def token_rows():
        lane = lax.broadcasted_iota(I32, (PART, PART), 1)
        sub = lax.broadcasted_iota(I32, (PART, PART), 0)

        def count(t, starts):
            row = tokens[pl.ds(t, 1), :].astype(F32)
            col = jnp.broadcast_to(row, (PART, PART)).T.astype(I32)
            nat[t] = col
            return starts + jnp.sum(jnp.where(col < lane, 1.0, 0.0), axis=0, keepdims=True)

        starts = lax.fori_loop(0, ZED, count, jnp.zeros((1, PART), F32))

        def place(t, carry):
            col = nat[t]
            begin = jnp.sum(jnp.where(col == lane, starts, 0.0), axis=1, keepdims=True)
            slot = t * PART + sub - begin.astype(I32)
            nat[t] = col * SLOTS + slot
            core = col & 1
            cx = (col >> 1) & 3
            cy = col >> 3
            q1 = jnp.where(core == 0, cx, cy)
            dist = jnp.where(core == 0, cy - y, cx - x) & 3
            group = jnp.where(dist == 2, 3, jnp.where(dist == 3, 2, dist))
            rel[t] = (group * 8 + core * 4 + q1) * SLOTS + slot
            return carry

        lax.fori_loop(0, ZED, place, 0)

    def one_hot(where, t, row):
        col = where[t]
        lane = lax.broadcasted_iota(I32, (PART, PART), 1)
        for c in range(SEQS * SLOTS // PART):
            hot[row:row + PART, c * PART:(c + 1) * PART] = jnp.where(
                col == lane + c * PART, 1.0, 0.0
            ).astype(BF16)

    token_rows()

    def second_sends(i):
        send(f"h{i}+", block(0, i), block(2, i), second(1))
        send(f"h{i}-", block(0, i), block(1, i), second(-1))

    arrived("g1+", block(0, 1))
    send("g2+", block(0, 1).at[:, lo], block(0, 1).at[:, lo], first(1))
    arrived("g1-", block(0, 2))
    send("g2-", block(0, 2).at[:, hi], block(0, 2).at[:, hi], first(-1))
    keep.wait()
    second_sends(0)
    second_sends(1)
    second_sends(2)
    send("s01", block(0, 1), block(0, 1), sibling)
    send("s02", block(0, 2), block(0, 2), sibling)

    def z_hop(h):
        if h < 3:
            arrived(f"a+{h}", abuf.at[ring8(z - h)])
            send(f"a+{h + 1}", abuf.at[ring8(z - h)], abuf.at[ring8(z - h)], along_z(1))
            arrived(f"a-{h}", abuf.at[ring8(z + h)])
            send(f"a-{h + 1}", abuf.at[ring8(z + h)], abuf.at[ring8(z + h)], along_z(-1))
        else:
            a, b = pl.ds(0, 2), pl.ds(2, 2)
            arrived("a+3", abuf.at[ring8(z - 3)])
            send("a+4", abuf.at[ring8(z - 3), a], abuf.at[ring8(z - 3), a], along_z(1))
            arrived("a-3", abuf.at[ring8(z + 3)])
            send("a-4", abuf.at[ring8(z + 3), b], abuf.at[ring8(z + 3), b], along_z(-1))

    z_hop(1)
    z_hop(2)
    arrived("g2+", block(0, 3).at[:, lo])
    arrived("g2-", block(0, 3).at[:, hi])
    second_sends(3)
    send("s03", block(0, 3), block(0, 3), sibling)
    z_hop(3)

    def pass_on(i):
        arrived(f"h{i}+", block(2, i))
        send(f"i{i}+", block(2, i).at[:, lo], block(3, i).at[:, lo], second(1))
        arrived(f"h{i}-", block(1, i))
        send(f"i{i}-", block(1, i).at[:, hi], block(3, i).at[:, hi], second(-1))
        send(f"s1{i}", block(1, i), block(1, i), sibling)
        send(f"s2{i}", block(2, i), block(2, i), sibling)

    def opposite(i):
        arrived(f"i{i}+", block(3, i).at[:, lo])
        arrived(f"i{i}-", block(3, i).at[:, hi])
        send(f"s3{i}", block(3, i), block(3, i), sibling)

    def rotate_grads(j):
        rows = gbuf[j].reshape(8 * SLOTS, wout.shape[0])
        for n in range(0, dout, 256):
            width = min(256, dout - n)
            res = jnp.dot(rows, wout[:, n:n + width], preferred_element_type=F32)
            top = res.astype(BF16)
            hilo[j * 384:(j + 1) * 384, n:n + width] = top
            hilo[j * 384:(j + 1) * 384, dout + n:dout + n + width] = (
                res - top.astype(F32)
            ).astype(BF16)

    pass_on(0)
    for i in range(4):
        arrived(f"s0{i}", sibling_block(0, i))
    load_out.wait()
    rotate_grads(0)
    opposite(0)

    arrived("a+4", abuf.at[ring8(z + 4), pl.ds(0, 2)])
    arrived("a-4", abuf.at[ring8(z + 4), pl.ds(2, 2)])
    keep_acts.wait()
    load_in.wait()

    def rotate_acts(p):
        one_hot(nat, 2 * p, 0)
        one_hot(nat, 2 * p + 1, PART)
        slots = abuf[...].reshape(SEQS * SLOTS, abuf.shape[-1])
        rows = jnp.dot(hot[...], slots, preferred_element_type=F32).astype(BF16)
        res = jnp.dot(rows, win[...], preferred_element_type=F32)
        rap[pl.ds(p * 8, 8)] = res.reshape(8, 32, res.shape[-1])

    lax.fori_loop(0, 2, lambda n, c: (rotate_acts(o * 2 + n), c)[1], 0)
    send("pair", rap.at[pl.ds(o * 16, 16)], pair_in, sibling)
    pass_on(1)
    lax.fori_loop(0, 2, lambda n, c: (rotate_acts(k * 2 + n), c)[1], 0)
    opposite(1)
    pass_on(2)
    arrived("pair", pair_in)
    base = k * 16
    def add_pair(n, c):
        rap[base + n] += pair_in[n]
        return c
    lax.fori_loop(0, 16, add_pair, 0)
    opposite(2)
    pass_on(3)

    def quarter(d):
        return base + ring4(p1 + d) * 4

    send("e1+", rap.at[pl.ds(quarter(2), 2)], e1_half.at[0], first(1))
    send("e1-", rap.at[pl.ds(quarter(2) + 2, 2)], e1_half.at[1], first(-1))

    for j in (1, 2):
        for i in range(4):
            arrived(f"s{j}{i}", sibling_block(j, i))
        rotate_grads(j)
    opposite(3)

    def e1_second_step():
        arrived("e1+", e1_half.at[0])
        rap[pl.ds(quarter(1), 2)] += e1_half[0]
        send("e2+", rap.at[pl.ds(quarter(1), 4)], e1_full.at[0], first(1))
        arrived("e1-", e1_half.at[1])
        rap[pl.ds(quarter(-1) + 2, 2)] += e1_half[1]
        send("e2-", rap.at[pl.ds(quarter(-1), 4)], e1_full.at[1], first(-1))

    e1_second_step()
    for i in range(4):
        arrived(f"s3{i}", sibling_block(3, i))
    rotate_grads(3)

    def compact(ds):
        for n, d in enumerate(ds):
            one_hot(rel, ring8(z + d), n * PART)
        rows = len(ds) * PART
        for n in range(0, dout, 256):
            width = min(256, dout - n)
            res = jnp.dot(hot[:rows], hilo[:, n:n + width], preferred_element_type=F32)
            res += jnp.dot(
                hot[:rows], hilo[:, dout + n:dout + n + width], preferred_element_type=F32
            )
            for m, d in enumerate(ds):
                parts[ring8(z + d), :, n:n + width] = res[m * PART:(m + 1) * PART]

    A, B = pl.ds(0, HALF), pl.ds(HALF, HALF)

    def c_send(direction, h, part):
        s = 1 if direction == 0 else -1
        rows = parts.at[ring8(z + s * h), B if part else A]
        send(f"c{direction}{h}{part}", rows, arrivals.at[direction, 2 * (4 - h) + part], along_z(s))

    def c_take(direction, h, part):
        s = 1 if direction == 0 else -1
        slot = arrivals.at[direction, 2 * (3 - h) + part]
        arrived(f"c{direction}{h + 1}{part}", slot)
        rows = pl.ds(part * HALF, HALF)
        parts[ring8(z + s * h), rows, :] += arrivals[direction, 2 * (3 - h) + part]

    compact((4,))
    c_send(0, 4, 0)
    c_send(1, 4, 1)
    compact((3, -3))
    c_send(0, 3, 1)
    c_send(1, 3, 0)

    def hop(h, fresh):
        for direction in (0, 1):
            part = fresh if direction == 0 else 1 - fresh
            c_take(direction, h, part)
            c_send(direction, h, part)

    arrived("e2+", e1_full.at[0])
    arrived("e2-", e1_full.at[1])
    rap[pl.ds(quarter(0), 4)] += e1_full[0] + e1_full[1]
    mid = quarter(0)

    def eighth(d):
        return mid + ring4(p2 + d)

    top, low = pl.ds(0, 16), pl.ds(16, 16)
    send("f1+", rap.at[eighth(2), top], e2_half.at[0], second(1))
    send("f1-", rap.at[eighth(2), low], e2_half.at[1], second(-1))
    hop(3, 0)
    compact((2, -2))
    arrived("f1+", e2_half.at[0])
    rap[eighth(1), 0:16] += e2_half[0]
    send("f2+", rap.at[eighth(1)], e2_full.at[0], second(1))
    arrived("f1-", e2_half.at[1])
    rap[eighth(-1), 16:32] += e2_half[1]
    send("f2-", rap.at[eighth(-1)], e2_full.at[1], second(-1))
    hop(2, 1)
    arrived("f2+", e2_full.at[0])
    arrived("f2-", e2_full.at[1])
    rot_acts[eighth(0)] = (rap[eighth(0)] + e2_full[0] + e2_full[1]).astype(BF16)
    send("j1+", rot_acts.at[eighth(0)], rot_acts.at[eighth(0)], second(1))
    send("j1-", rot_acts.at[eighth(0)], rot_acts.at[eighth(0)], second(-1))
    compact((1, -1))
    hop(2, 0)
    arrived("j1+", rot_acts.at[eighth(-1)])
    send("j2+", rot_acts.at[eighth(-1), top], rot_acts.at[eighth(-1), top], second(1))
    arrived("j1-", rot_acts.at[eighth(1)])
    send("j2-", rot_acts.at[eighth(1), low], rot_acts.at[eighth(1), low], second(-1))
    compact((0,))
    arrived("j2+", rot_acts.at[eighth(2), top])
    arrived("j2-", rot_acts.at[eighth(2), low])

    def quarter_rows(d):
        return rot_acts.at[pl.ds(quarter(d), 4)]

    send("k1+", quarter_rows(0), quarter_rows(0), first(1))
    send("k1-", quarter_rows(0), quarter_rows(0), first(-1))
    send("t0", quarter_rows(0), quarter_rows(0), sibling)
    hop(1, 1)
    arrived("k1+", quarter_rows(-1))
    send("k2+", rot_acts.at[pl.ds(quarter(-1), 2)], rot_acts.at[pl.ds(quarter(-1), 2)], first(1))
    arrived("k1-", quarter_rows(1))
    send("k2-", rot_acts.at[pl.ds(quarter(1) + 2, 2)], rot_acts.at[pl.ds(quarter(1) + 2, 2)], first(-1))
    send("t1", quarter_rows(-1), quarter_rows(-1), sibling)
    send("t2", quarter_rows(1), quarter_rows(1), sibling)
    hop(1, 0)
    arrived("k2+", rot_acts.at[pl.ds(quarter(2), 2)])
    arrived("k2-", rot_acts.at[pl.ds(quarter(2) + 2, 2)])
    send("t3", quarter_rows(2), quarter_rows(2), sibling)
    for i, d in enumerate(OFFSETS):
        arrived(f"t{i}", rot_acts.at[pl.ds(o * 16 + ring4(p2 + d) * 4, 4)])
    load_q.wait()

    def project(t, carry):
        rows = rot_acts[pl.ds(t * 8, 8)].reshape(256, rot_acts.shape[-1])
        for q in range(2):
            res = lax.dot_general(
                rows, wq[q], (((1,), (1,)), ((), ())), preferred_element_type=F32
            )
            proj[pl.ds(2 * t, 2), q] = res.reshape(2, PART, dout)
        return carry

    lax.fori_loop(0, 4, project, 0)

    for part in (1, 0):
        rows = pl.ds(part * HALF, HALF)
        for direction in (0, 1):
            c_take(direction, 0, part)
        rot_grads[z, rows, :] = parts[z, rows, :].astype(BF16)
        for direction, s in ((0, 1), (1, -1)):
            ref = rot_grads.at[z, B if part else A]
            send(f"d{direction}1{part}", ref, ref, along_z(s))

    def score(t):
        tile = jnp.zeros((8, PART), F32)
        line = lax.broadcasted_iota(I32, (8, PART), 0)
        for q in range(2):
            total = jnp.zeros((PART, PART), F32)
            for n in range(0, dout, PART):
                total += rot_grads[t, :, n:n + PART].astype(F32) * proj[t, q, :, n:n + PART]
            sums = jnp.sum(total.T, axis=0, keepdims=True)
            tile = jnp.where(line == q, sums, tile)
        mine[t] = tile

    def give_score(d):
        t = ring8(z + d)
        score(t)
        send(f"z{d % 8}", mine.at[t], zsum.at[z], along_z(d))

    score(z)
    for h in (1, 2, 3):
        for part in (1, 0):
            for direction, s in ((0, 1), (1, -1)):
                ref = rot_grads.at[ring8(z - s * h), B if part else A]
                arrived(f"d{direction}{h}{part}", ref)
                if h < 3 or part == direction:
                    send(f"d{direction}{h + 1}{part}", ref, ref, along_z(s))
        give_score(-h)
        give_score(h)
    arrived("d040", rot_grads.at[ring8(z + 4), A])
    arrived("d141", rot_grads.at[ring8(z + 4), B])
    give_score(4)

    total = mine[z]
    for d in range(1, 8):
        src = ring8(z - d)
        arrived(f"z{d}", zsum.at[src])
        total += zsum[src]
    plane[0] = total
    send("core", plane.at[0], plane.at[1], sibling)
    arrived("core", plane.at[1])
    plane[2] = plane[0] + plane[1]
    for d in (1, 2, 3):
        send(f"x{d}", plane.at[2], plane.at[2 + d], along_x(d))
    for d in (1, 2, 3):
        arrived(f"x{d}", plane.at[2 + d])
    plane[6] = plane[2] + plane[3] + plane[4] + plane[5]
    for d in (1, 2, 3):
        send(f"y{d}", plane.at[6], plane.at[6 + d], along_y(d))
    for d in (1, 2, 3):
        arrived(f"y{d}", plane.at[6 + d])
    total = plane[6] + plane[7] + plane[8] + plane[9]
    c = (y * 4 + x) * 2 + k
    lane = lax.broadcasted_iota(I32, (8, PART), 1)
    line = lax.broadcasted_iota(I32, (8, PART), 0)
    pick = lane == c * 4 + line
    cols = [
        jnp.sum(jnp.where(pick, jnp.broadcast_to(total[q:q + 1], (8, PART)), 0.0), axis=1, keepdims=True)
        for q in range(2)
    ]
    both = jnp.where(lane == 0, cols[0], cols[1])
    out[...] = both[0:4, 0:2]

    for copy in started:
        copy.wait_send()
    assert len(ids) <= N_SEMS


def local(out_grads, acts, rot_out, rot_in, queries, token_sequence):
    din_r, dout_c = rot_out.shape
    din_c, din_z = rot_in.shape
    any_ref = pl.BlockSpec(memory_space=pl.ANY)
    vmem = pl.BlockSpec(memory_space=pltpu.VMEM)
    scratch = [
        pltpu.VMEM((4, 8, SLOTS, din_r), BF16),
        pltpu.VMEM((din_r, dout_c), BF16),
        pltpu.VMEM((din_c, din_z), BF16),
        pltpu.VMEM(queries.shape, BF16),
        pltpu.VMEM((SEQS * SLOTS, 2 * dout_c), BF16),
        pltpu.VMEM((ZED, PART, dout_c), F32),
        pltpu.VMEM((2, 8, HALF, dout_c), F32),
        pltpu.VMEM((ZED, PART, dout_c), BF16),
        pltpu.VMEM((ZED, 4, SLOTS, din_c), BF16),
        pltpu.VMEM((32, 32, din_z), F32),
        pltpu.VMEM((16, 32, din_z), F32),
        pltpu.VMEM((2, 2, 32, din_z), F32),
        pltpu.VMEM((2, 4, 32, din_z), F32),
        pltpu.VMEM((2, 16, din_z), F32),
        pltpu.VMEM((2, 32, din_z), F32),
        pltpu.VMEM((32, 32, din_z), BF16),
        pltpu.VMEM((ZED, 2, PART, dout_c), F32),
        pltpu.VMEM((2 * PART, SEQS * SLOTS), BF16),
        pltpu.VMEM((ZED, PART, PART), I32),
        pltpu.VMEM((ZED, PART, PART), I32),
        pltpu.VMEM((ZED, 8, PART), F32),
        pltpu.VMEM((ZED, 8, PART), F32),
        pltpu.VMEM((10, 8, PART), F32),
        pltpu.SemaphoreType.DMA((N_SEMS,)),
        pltpu.SemaphoreType.DMA((N_SEMS,)),
        pltpu.SemaphoreType.DMA((5,)),
    ]
    return pl.pallas_call(
        kernel,
        out_shape=jax.ShapeDtypeStruct((4, 2), F32),
        in_specs=[any_ref] * 5 + [vmem],
        out_specs=vmem,
        scratch_shapes=scratch,
        compiler_params=pltpu.CompilerParams(
            collective_id=0, has_side_effects=True, vmem_limit_bytes=62 * 1024 * 1024
        ),
        name="influence",
    )(out_grads, acts, rot_out, rot_in, queries, token_sequence.reshape(8, 128))


def solution(mesh):
    torus = Mesh(
        mesh.devices.reshape(mesh.shape["row"], 4, 4, 2), ("row", "col_0", "col_1", "col_2")
    )
    in_specs = (
        P(COL, None, "row"),
        P("row", None, COL),
        P("row", COL),
        P(COL, "row"),
        P(None, COL, "row"),
        P(),
    )
    out_specs = P(ROW_COL, None)
    return jax.shard_map(local, mesh=torus, in_specs=in_specs, out_specs=out_specs, check_vma=False)
```

```python
import jax
import jax.numpy as jnp
from jax import lax
from jax.experimental import pallas as pl
from jax.experimental.pallas import tpu as pltpu
from jax.sharding import Mesh
from jax.sharding import PartitionSpec as P

COL = ("col_0", "col_1", "col_2")
ROW_COL = ("row", "col_0", "col_1", "col_2")
MESH = pl.DeviceIdType.MESH
F32 = jnp.float32
BF16 = jnp.bfloat16
I32 = jnp.int32

RING = 4
ZED = 8
SLOTS = 48
SEQS = 32
PART = 128
HALF = 64
SUB = 32
OFFSETS = (0, -1, 1, 2)
OFFSETS2 = (0, 1, -1, 2)
PLACES = (
    (0, 0), (0, 1), (0, 2), (0, 3), (1, 0), (2, 0), (1, 1), (2, 1),
    (3, 0), (1, 2), (2, 2), (3, 1), (1, 3), (2, 3), (3, 2), (3, 3),
)
N_SEMS = 123
EARLY = 12 * 2 * SLOTS
LATE = 8 * SLOTS
KINDS = "gashicdepfjktzxy"


def ring4(i):
    return lax.rem(i + 8, 4)


def ring8(i):
    return lax.rem(i + 16, 8)


def kernel(
    grads, acts, rot_out_hbm, rot_in_hbm, queries_hbm, tokens, out,
    gbuf, wout, win, wq, hilo, parts, arrivals, rot_grads, abuf, rap, pair_in,
    e1_half, e1_full, e2_half, e2_full, rot_acts, proj, hot, order, nat, rel, perm, lanes, mine, zsum, plane,
    send_sems, recv_sems, local_sems,
):
    z = lax.axis_index("row")
    y = lax.axis_index("col_0")
    x = lax.axis_index("col_1")
    k = lax.axis_index("col_2")
    o = 1 - k
    p1 = x * o + y * k
    p2 = y * o + x * k
    dout = wout.shape[1]
    half_in = wout.shape[0] // 2

    def first(d):
        return (z, ring4(y + k * d), ring4(x + o * d), k)

    def second(d):
        return (z, ring4(y + o * d), ring4(x + k * d), k)

    def along_z(d):
        return (ring8(z + d), y, x, k)

    sibling = (z, y, x, o)

    def along_x(d):
        return (z, y, ring4(x + d), k)

    def along_y(d):
        return (z, ring4(y + d), x, k)

    peers = [sibling] + [along_z(d) for d in range(1, 8)]
    peers += [along_x(d) for d in (1, 2, 3)] + [along_y(d) for d in (1, 2, 3)]
    barrier = pltpu.get_barrier_semaphore()
    for peer in peers:
        pl.semaphore_signal(barrier, inc=1, device_id=peer, device_id_type=MESH)

    ids = {}

    def sem_id(name):
        return ids.setdefault(name, len(ids))

    def send(name, src, dst, to):
        kind = KINDS.index(name[0])
        pltpu.make_async_remote_copy(
            src_ref=src, dst_ref=dst, send_sem=send_sems.at[kind],
            recv_sem=recv_sems.at[sem_id(name)], device_id=to, device_id_type=MESH,
        ).start()

    def sent(kind, ref):
        pltpu.make_async_remote_copy(
            src_ref=ref, dst_ref=ref, send_sem=send_sems.at[KINDS.index(kind)],
            recv_sem=recv_sems.at[0], device_id=sibling, device_id_type=MESH,
        ).wait_send()

    def arrived(name, dst):
        i = sem_id(name)
        pltpu.make_async_remote_copy(
            src_ref=dst, dst_ref=dst, send_sem=send_sems.at[0], recv_sem=recv_sems.at[i],
            device_id=sibling, device_id_type=MESH,
        ).wait_recv()

    lo, hi = pl.ds(0, half_in), pl.ds(half_in, half_in)

    def block(j, i):
        return gbuf.at[PLACES.index((j, i)), k]

    def sibling_block(j, i):
        return gbuf.at[PLACES.index((j, i)), o]

    own = grads.at[0]
    keep = pltpu.make_async_copy(own, block(0, 0), local_sems.at[0])
    keep_acts = pltpu.make_async_copy(acts, abuf.at[z], local_sems.at[1])
    load_in = pltpu.make_async_copy(rot_in_hbm, win, local_sems.at[2])
    load_out = pltpu.make_async_copy(rot_out_hbm, wout, local_sems.at[3])
    load_q = pltpu.make_async_copy(queries_hbm, wq, local_sems.at[4])
    for copy in (keep, keep_acts, load_in, load_out, load_q):
        copy.start()

    def token_rows():
        lane = lax.broadcasted_iota(I32, (PART, PART), 1)
        sub = lax.broadcasted_iota(I32, (PART, PART), 0)

        def place_of(core, seq_y, seq_x):
            near = jnp.where(core == 0, seq_x - x, seq_y - y) & 3
            far = jnp.where(core == 0, seq_y - y, seq_x - x) & 3
            where = far * 4 + near
            at = jnp.zeros_like(where)
            for place, (j, i) in enumerate(PLACES):
                at = jnp.where(where == (OFFSETS2[j] % 4) * 4 + OFFSETS[i] % 4, place, at)
            return at * 2 + core

        head = lax.broadcasted_iota(I32, (8, PART), 1)
        core, at = head & 1, head >> 1
        near, far = jnp.zeros_like(at), jnp.zeros_like(at)
        for place, (j, i) in enumerate(PLACES):
            near = jnp.where(at == place, OFFSETS[i], near)
            far = jnp.where(at == place, OFFSETS2[j], far)
        seq_x = jnp.where(core == 0, near, far) + x
        seq_y = jnp.where(core == 0, far, near) + y
        held = ((seq_y & 3) * 8 + (seq_x & 3) * 2 + core)[0:1]

        def count(t, sums):
            row = tokens[pl.ds(t, 1), :].astype(F32)
            col = jnp.broadcast_to(row, (PART, PART)).T.astype(I32)
            nat[t] = col
            rank = place_of(col & 1, col >> 3, (col >> 1) & 3)
            return tuple(
                old + jnp.sum(jnp.where(mark, 1.0, 0.0), axis=0, keepdims=True)
                for old, mark in zip(sums, (col < lane, rank < lane, col < held))
            )

        zero = jnp.zeros((1, PART), F32)
        begins, ranked, origin = lax.fori_loop(0, ZED, count, (zero, zero, zero))

        def place(t, carry):
            col = nat[t]
            begin = jnp.sum(jnp.where(col == lane, begins, 0.0), axis=1, keepdims=True)
            nat[t] = col * SLOTS + t * PART + sub - begin.astype(I32)
            u = (sub >> 6) * 512 + t * HALF + (sub & (HALF - 1))
            before = ranked <= u.astype(F32)
            rank = jnp.sum(jnp.where(before, 1.0, 0.0), axis=1, keepdims=True) - 1.0
            start = jnp.max(jnp.where(before, ranked, 0.0), axis=1, keepdims=True)
            first_of = jnp.sum(
                jnp.where(lane.astype(F32) == rank, origin, 0.0), axis=1, keepdims=True
            )
            slot = u - start.astype(I32)
            rel[t] = rank.astype(I32) * SLOTS + slot
            perm[t] = first_of.astype(I32) + slot
            return carry

        lax.fori_loop(0, ZED, place, 0)

    def one_hot(target, row, where, low, high):
        count = where.shape[0]
        lane = lax.broadcasted_iota(I32, (count, PART), 1)
        for c in range(low // PART, high // PART):
            target[row:row + count, c * PART:(c + 1) * PART] = jnp.where(
                where == lane + c * PART, 1.0, 0.0
            ).astype(BF16)

    token_rows()

    pl.semaphore_wait(barrier, len(peers))

    send("g1+", own, block(0, 1), first(1))
    send("g1-", own, block(0, 2), first(-1))
    send("s00", own, block(0, 0), sibling)
    send("a+1", acts, abuf.at[z], along_z(1))
    send("a-1", acts, abuf.at[z], along_z(-1))

    def second_sends(i, src=None):
        src = block(0, i) if src is None else src
        send(f"h{i}+", src, block(2, i), second(1))
        send(f"h{i}-", src, block(1, i), second(-1))

    def z_hop(h):
        for sign, s, part in (("+", 1, 0), ("-", -1, 2)):
            ref = abuf.at[ring8(z - s * h)]
            arrived(f"a{sign}{h}", ref)
            ref = ref if h < 3 else ref.at[pl.ds(part, 2)]
            send(f"a{sign}{h + 1}", ref, ref, along_z(s))

    def pass_on(i):
        arrived(f"h{i}+", block(2, i))
        send(f"i{i}+", block(2, i).at[:, lo], block(3, i).at[:, lo], second(1))
        arrived(f"h{i}-", block(1, i))
        send(f"i{i}-", block(1, i).at[:, hi], block(3, i).at[:, hi], second(-1))
        send(f"s1{i}", block(1, i), block(1, i), sibling)
        send(f"s2{i}", block(2, i), block(2, i), sibling)

    def opposite(i):
        arrived(f"i{i}+", block(3, i).at[:, lo])
        arrived(f"i{i}-", block(3, i).at[:, hi])
        send(f"s3{i}", block(3, i), block(3, i), sibling)

    def rotate_grads(start, stop):
        for j, i in PLACES[start:stop]:
            arrived(f"s{j}{i}", sibling_block(j, i))
        rows = gbuf[start:stop].reshape((stop - start) * 2 * SLOTS, wout.shape[0])
        at = slice(start * 2 * SLOTS, stop * 2 * SLOTS)
        for n in range(0, dout, 256):
            width = min(256, dout - n)
            res = jnp.dot(rows, wout[:, n:n + width], preferred_element_type=F32)
            top = res.astype(BF16)
            hilo[at, n:n + width] = top
            hilo[at, dout + n:dout + n + width] = (res - top.astype(F32)).astype(BF16)

    def rotate_acts(p):
        one_hot(hot, 0, nat[2 * p], 0, SEQS * SLOTS)
        one_hot(hot, PART, nat[2 * p + 1], 0, SEQS * SLOTS)
        slots = abuf[...].reshape(SEQS * SLOTS, abuf.shape[-1])
        rows = jnp.dot(hot[:2 * PART], slots, preferred_element_type=F32).astype(BF16)
        res = jnp.dot(rows, win[...], preferred_element_type=F32)
        rap[pl.ds(p * 8, 8)] = res.reshape(8, 32, res.shape[-1])

    second_sends(0, own)
    arrived("g1+", block(0, 1))
    send("g2+", block(0, 1).at[:, lo], block(0, 3).at[:, lo], first(1))
    arrived("g1-", block(0, 2))
    send("g2-", block(0, 2).at[:, hi], block(0, 3).at[:, hi], first(-1))
    second_sends(1)
    second_sends(2)
    send("s01", block(0, 1), block(0, 1), sibling)
    send("s02", block(0, 2), block(0, 2), sibling)
    z_hop(1)
    keep.wait()
    load_out.wait()
    pass_on(0)
    z_hop(2)
    arrived("g2+", block(0, 3).at[:, lo])
    arrived("g2-", block(0, 3).at[:, hi])
    second_sends(3)
    send("s03", block(0, 3), block(0, 3), sibling)
    def compact(ds, half):
        low, high = (0, EARLY) if half == 0 else (LATE, SEQS * SLOTS)
        rows = slice(half * HALF, (half + 1) * HALF)
        for n, d in enumerate(ds):
            one_hot(hot, n * HALF, rel[ring8(z + d), rows], low, high)
        picks = hot[:len(ds) * HALF, low:high]
        for n in range(0, dout, 256):
            width = min(256, dout - n)
            res = jnp.dot(picks, hilo[low:high, n:n + width], preferred_element_type=F32)
            res += jnp.dot(
                picks, hilo[low:high, dout + n:dout + n + width], preferred_element_type=F32
            )
            for m, d in enumerate(ds):
                parts[ring8(z + d), rows, n:n + width] = res[m * HALF:(m + 1) * HALF]

    SIGNS = (1, -1)

    def c_send(half, direction, h, sub):
        s = SIGNS[direction]
        rows = parts.at[ring8(z + s * h), pl.ds(half * HALF + sub * SUB, SUB)]
        slot = arrivals.at[half, direction, 2 * (4 - h) + sub]
        send(f"c{half}{direction}{h}{sub}", rows, slot, along_z(s))

    def c_take(half, direction, h, sub):
        s = SIGNS[direction]
        at = 2 * (3 - h) + sub
        arrived(f"c{half}{direction}{h + 1}{sub}", arrivals.at[half, direction, at])
        rows = pl.ds(half * HALF + sub * SUB, SUB)
        parts[ring8(z + s * h), rows, :] += arrivals[half, direction, at]

    def c_open(half):
        c_send(half, 0, 4, 0)
        c_send(half, 1, 4, 1)
        c_send(half, 0, 3, 1)
        c_send(half, 1, 3, 0)

    def hop(half, h, fresh):
        for direction in (0, 1):
            sub = fresh if direction == 0 else 1 - fresh
            c_take(half, direction, h, sub)
            c_send(half, direction, h, sub)

    def d_ref(half, d):
        return rot_grads.at[ring8(z + d), pl.ds(half * HALF, HALF)]

    def c_close(half):
        for sub in (1, 0):
            for direction in (0, 1):
                c_take(half, direction, 0, sub)
        rows = pl.ds(half * HALF, HALF)
        rot_grads[z, rows, :] = parts[z, rows, :].astype(BF16)
        for direction, s in enumerate(SIGNS):
            send(f"d{half}{direction}1", d_ref(half, 0), d_ref(half, 0), along_z(s))

    def d_hop(half, h):
        for direction, s in enumerate(SIGNS):
            ref = d_ref(half, -s * h)
            if h < 4:
                arrived(f"d{half}{direction}{h}", ref)
            if h == 3:
                ref = ref.at[pl.ds(direction * SUB, SUB)]
            if h == 4:
                ref = ref.at[pl.ds(direction * SUB, SUB)]
                arrived(f"d{half}{direction}{h}", ref)
            else:
                send(f"d{half}{direction}{h + 1}", ref, ref, along_z(s))

    rotate_grads(0, 3)
    z_hop(3)
    pass_on(1)
    opposite(0)
    arrived("a+4", abuf.at[ring8(z + 4), pl.ds(0, 2)])
    arrived("a-4", abuf.at[ring8(z + 4), pl.ds(2, 2)])
    keep_acts.wait()
    load_in.wait()
    lax.fori_loop(0, 2, lambda n, c: (rotate_acts(o * 2 + n), c)[1], 0)
    send("pair", rap.at[pl.ds(o * 16, 16)], pair_in, sibling)
    rotate_grads(3, 8)
    pass_on(2)
    opposite(1)
    rotate_grads(8, 12)
    compact((4, 3, -3), 0)
    c_open(0)
    pass_on(3)
    opposite(2)
    compact((2, -2, 1, -1, 0), 0)
    hop(0, 3, 0)
    lax.fori_loop(0, 2, lambda n, c: (rotate_acts(k * 2 + n), c)[1], 0)
    arrived("pair", pair_in)
    base = k * 16

    def add_pair(n, c):
        rap[base + n] += pair_in[n]
        return c

    lax.fori_loop(0, 16, add_pair, 0)

    def quarter(d):
        return base + ring4(p1 + d) * 4

    send("e1+", rap.at[pl.ds(quarter(2), 2)], e1_half.at[0], first(1))
    send("e1-", rap.at[pl.ds(quarter(2) + 2, 2)], e1_half.at[1], first(-1))
    hop(0, 2, 1)
    opposite(3)
    rotate_grads(12, 15)
    hop(0, 2, 0)
    arrived("e1+", e1_half.at[0])
    rap[pl.ds(quarter(1), 2)] += e1_half[0]
    send("e2+", rap.at[pl.ds(quarter(1), 4)], e1_full.at[0], first(1))
    arrived("e1-", e1_half.at[1])
    rap[pl.ds(quarter(-1) + 2, 2)] += e1_half[1]
    send("e2-", rap.at[pl.ds(quarter(-1), 4)], e1_full.at[1], first(-1))
    rotate_grads(15, 16)
    hop(0, 1, 1)
    compact((4, 3, -3), 1)
    c_open(1)
    hop(0, 1, 0)
    arrived("e2+", e1_full.at[0])
    arrived("e2-", e1_full.at[1])
    rap[pl.ds(quarter(0), 4)] += e1_full[0] + e1_full[1]
    mid = quarter(0)

    def eighth(d):
        return mid + ring4(p2 + d)

    top, low = pl.ds(0, 16), pl.ds(16, 16)
    send("f1+", rap.at[eighth(2), top], e2_half.at[0], second(1))
    send("f1-", rap.at[eighth(2), low], e2_half.at[1], second(-1))
    compact((2, -2, 1, -1, 0), 1)
    hop(1, 3, 0)
    c_close(0)
    arrived("f1+", e2_half.at[0])
    rap[eighth(1), 0:16] += e2_half[0]
    send("f2+", rap.at[eighth(1)], e2_full.at[0], second(1))
    arrived("f1-", e2_half.at[1])
    rap[eighth(-1), 16:32] += e2_half[1]
    send("f2-", rap.at[eighth(-1)], e2_full.at[1], second(-1))
    hop(1, 2, 1)
    arrived("f2+", e2_full.at[0])
    arrived("f2-", e2_full.at[1])
    rot_acts[eighth(0)] = (rap[eighth(0)] + e2_full[0] + e2_full[1]).astype(BF16)
    send("j1+", rot_acts.at[eighth(0)], rot_acts.at[eighth(0)], second(1))
    send("j1-", rot_acts.at[eighth(0)], rot_acts.at[eighth(0)], second(-1))

    def fill_order(t, carry):
        one_hot(order.at[t], 0, perm[t], 0, ZED * PART)
        return carry

    lax.fori_loop(0, ZED, fill_order, 0)
    hop(1, 2, 0)
    d_hop(0, 1)
    arrived("j1+", rot_acts.at[eighth(-1)])
    send("j2+", rot_acts.at[eighth(-1), top], rot_acts.at[eighth(-1), top], second(1))
    arrived("j1-", rot_acts.at[eighth(1)])
    send("j2-", rot_acts.at[eighth(1), low], rot_acts.at[eighth(1), low], second(-1))
    hop(1, 1, 1)
    arrived("j2+", rot_acts.at[eighth(2), top])
    arrived("j2-", rot_acts.at[eighth(2), low])

    def quarter_rows(d):
        return rot_acts.at[pl.ds(quarter(d), 4)]

    send("k1+", quarter_rows(0), quarter_rows(0), first(1))
    send("k1-", quarter_rows(0), quarter_rows(0), first(-1))
    send("t0", quarter_rows(0), quarter_rows(0), sibling)
    hop(1, 1, 0)
    d_hop(0, 2)
    arrived("k1+", quarter_rows(-1))
    ref = rot_acts.at[pl.ds(quarter(-1), 2)]
    send("k2+", ref, ref, first(1))
    arrived("k1-", quarter_rows(1))
    ref = rot_acts.at[pl.ds(quarter(1) + 2, 2)]
    send("k2-", ref, ref, first(-1))
    send("t1", quarter_rows(-1), quarter_rows(-1), sibling)
    send("t2", quarter_rows(1), quarter_rows(1), sibling)
    c_close(1)
    d_hop(0, 3)
    arrived("k2+", rot_acts.at[pl.ds(quarter(2), 2)])
    arrived("k2-", rot_acts.at[pl.ds(quarter(2) + 2, 2)])
    send("t3", quarter_rows(2), quarter_rows(2), sibling)
    for i, d in enumerate(OFFSETS):
        arrived(f"t{i}", rot_acts.at[pl.ds(o * 16 + ring4(p2 + d) * 4, 4)])
    load_q.wait()

    def project(t):
        own_order = order[2 * t:2 * t + 2].reshape(2 * PART, ZED * PART)
        natural = rot_acts[...].reshape(ZED * PART, rot_acts.shape[-1])
        rows = jnp.dot(own_order, natural, preferred_element_type=F32).astype(BF16)
        for q in range(2):
            res = lax.dot_general(
                rows, wq[q], (((1,), (1,)), ((), ())), preferred_element_type=F32
            )
            proj[2 * t:2 * t + 2, q] = res.reshape(2, PART, dout)

    def multiply(t, half):
        rows = pl.ds(half * HALF, HALF)
        for q in range(2):
            total = jnp.zeros((HALF, PART), F32)
            for n in range(0, dout, PART):
                total += (
                    rot_grads[t, rows, n:n + PART].astype(F32) * proj[t, q, rows, n:n + PART]
                )
            lanes[t, q, rows, :] = total

    line = lax.broadcasted_iota(I32, (16, PART), 0)

    def in_token_order(t):
        tile = jnp.zeros((16, PART), F32)
        for q in range(2):
            rest = jnp.sum(lanes[t, q].T, axis=0, keepdims=True)
            for term in range(3):
                piece = rest.astype(BF16).astype(F32)
                tile = jnp.where(line == 2 * term + q, piece, tile)
                rest = rest - piece
        return jnp.dot(tile.astype(BF16), order[t], preferred_element_type=F32)

    project(0)
    project(1)
    d_hop(1, 1)
    project(2)
    d_hop(0, 4)
    project(3)
    d_hop(1, 2)

    def multiply_early(t, carry):
        multiply(t, 0)
        return carry

    lax.fori_loop(0, ZED, multiply_early, 0)
    multiply(z, 1)
    scores = in_token_order(z)
    for d in (1, -1, 2, -2):
        multiply(ring8(z + d), 1)
        scores += in_token_order(ring8(z + d))
    d_hop(1, 3)
    for d in (3, -3):
        multiply(ring8(z + d), 1)
        scores += in_token_order(ring8(z + d))
    d_hop(1, 4)
    multiply(ring8(z + 4), 1)
    scores += in_token_order(ring8(z + 4))
    scores = scores[0:8] + jnp.where(
        lax.broadcasted_iota(I32, scores[0:8].shape, 0) < 2,
        pltpu.roll(scores[0:8], 6, 0) + pltpu.roll(scores[0:8], 4, 0), 0.0
    )
    for t in range(ZED):
        mine[t] = scores[:, t * PART:(t + 1) * PART]
    for d in range(1, 8):
        send(f"z{d}", mine.at[ring8(z + d)], zsum.at[z], along_z(d))
    total = mine[z]
    for d in range(1, 8):
        src = ring8(z - d)
        arrived(f"z{d}", zsum.at[src])
        total += zsum[src]
    plane[0] = total
    send("xcore", plane.at[0], plane.at[1], sibling)
    arrived("xcore", plane.at[1])
    plane[2] = plane[0] + plane[1]
    for d in (1, 2, 3):
        send(f"x{d}", plane.at[2], plane.at[2 + d], along_x(d))
    for d in (1, 2, 3):
        arrived(f"x{d}", plane.at[2 + d])
    plane[6] = plane[2] + plane[3] + plane[4] + plane[5]
    for d in (1, 2, 3):
        send(f"y{d}", plane.at[6], plane.at[6 + d], along_y(d))
    for d in (1, 2, 3):
        arrived(f"y{d}", plane.at[6 + d])
    total = plane[6] + plane[7] + plane[8] + plane[9]
    c = (y * 4 + x) * 2 + k
    lane = lax.broadcasted_iota(I32, (8, PART), 1)
    row = lax.broadcasted_iota(I32, (8, PART), 0)
    pick = lane == c * 4 + row
    cols = [
        jnp.sum(
            jnp.where(pick, jnp.broadcast_to(total[q:q + 1], (8, PART)), 0.0),
            axis=1, keepdims=True,
        )
        for q in range(2)
    ]
    both = jnp.where(lane == 0, cols[0], cols[1])
    out[...] = both[0:4, 0:2]

    sent("g", gbuf.at[pl.ds(0, 3), 0])
    sent("a", abuf.at[pl.ds(0, 7)])
    sent("s", gbuf.at[pl.ds(0, 8)])
    sent("h", gbuf.at[pl.ds(0, 4)])
    sent("i", gbuf.at[pl.ds(0, 2)])
    sent("c", parts.at[pl.ds(0, 7)])
    sent("d", rot_grads.at[pl.ds(0, 7)])
    sent("e", rap.at[pl.ds(0, 12)])
    sent("p", pair_in)
    sent("f", rap.at[pl.ds(0, 3)])
    sent("j", rot_acts.at[pl.ds(0, 3)])
    sent("k", rot_acts.at[pl.ds(0, 12)])
    sent("t", rot_acts.at[pl.ds(0, 16)])
    sent("z", zsum.at[pl.ds(0, 7)])
    sent("x", plane.at[pl.ds(0, 4)])
    sent("y", plane.at[pl.ds(0, 3)])
    assert len(ids) == N_SEMS


def local(out_grads, acts, rot_out, rot_in, queries, token_sequence):
    din_r, dout_c = rot_out.shape
    din_c, din_z = rot_in.shape
    any_ref = pl.BlockSpec(memory_space=pl.ANY)
    vmem = pl.BlockSpec(memory_space=pltpu.VMEM)
    scratch = [
        pltpu.VMEM((16, 2, SLOTS, din_r), BF16),
        pltpu.VMEM((din_r, dout_c), BF16),
        pltpu.VMEM((din_c, din_z), BF16),
        pltpu.VMEM(queries.shape, BF16),
        pltpu.VMEM((SEQS * SLOTS, 2 * dout_c), BF16),
        pltpu.VMEM((ZED, PART, dout_c), F32),
        pltpu.VMEM((2, 2, 8, SUB, dout_c), F32),
        pltpu.VMEM((ZED, PART, dout_c), BF16),
        pltpu.VMEM((ZED, 4, SLOTS, din_c), BF16),
        pltpu.VMEM((32, 32, din_z), F32),
        pltpu.VMEM((16, 32, din_z), F32),
        pltpu.VMEM((2, 2, 32, din_z), F32),
        pltpu.VMEM((2, 4, 32, din_z), F32),
        pltpu.VMEM((2, 16, din_z), F32),
        pltpu.VMEM((2, 32, din_z), F32),
        pltpu.VMEM((32, 32, din_z), BF16),
        pltpu.VMEM((ZED, 2, PART, dout_c), F32),
        pltpu.VMEM((5 * HALF, SEQS * SLOTS), BF16),
        pltpu.VMEM((ZED, PART, ZED * PART), BF16),
        pltpu.VMEM((ZED, PART, PART), I32),
        pltpu.VMEM((ZED, PART, PART), I32),
        pltpu.VMEM((ZED, PART, PART), I32),
        pltpu.VMEM((ZED, 2, PART, PART), F32),
        pltpu.VMEM((ZED, 8, PART), F32),
        pltpu.VMEM((ZED, 8, PART), F32),
        pltpu.VMEM((10, 8, PART), F32),
        pltpu.SemaphoreType.DMA((len(KINDS),)),
        pltpu.SemaphoreType.DMA((N_SEMS,)),
        pltpu.SemaphoreType.DMA((5,)),
    ]
    return pl.pallas_call(
        kernel,
        out_shape=jax.ShapeDtypeStruct((4, 2), F32),
        in_specs=[any_ref] * 5 + [vmem],
        out_specs=vmem,
        scratch_shapes=scratch,
        compiler_params=pltpu.CompilerParams(
            collective_id=0, has_side_effects=True, vmem_limit_bytes=62 * 1024 * 1024
        ),
        name="influence",
    )(out_grads, acts, rot_out, rot_in, queries, token_sequence.reshape(8, 128))


def solution(mesh):
    torus = Mesh(
        mesh.devices.reshape(mesh.shape["row"], 4, 4, 2), ("row", "col_0", "col_1", "col_2")
    )
    in_specs = (
        P(COL, None, "row"),
        P("row", None, COL),
        P("row", COL),
        P(COL, "row"),
        P(None, COL, "row"),
        P(),
    )
    out_specs = P(ROW_COL, None)
    return jax.shard_map(local, mesh=torus, in_specs=in_specs, out_specs=out_specs, check_vma=False)
```
